32 devices in a mesh: exp: 8 (over y, x, core), seq: 4 (over z).
Axes of the slice: x: 2, y: 2, z: 4, core: 2. Of those that a mesh axis runs over, the one named last changes fastest.
Arguments:
- tokens: bfloat16 [8192, 768], P(('exp', 'seq')), may hold values from -6 to 6
- segments: int32 [8192], P('exp'), may hold values from 0 to 510, as said below
- expert_ids: int32 [8192, 2], P(('exp', 'seq')), may hold values from 0 to 15, all different within a row; in each aligned block of 256 rows (0 to 255, 256 to 511, ...) at most 39 rows name the same one
- gain_attn: bfloat16 [768], P(('exp', 'seq')), may hold values from 0.099609375 to 1.8984375
- attn_in: bfloat16 [768, 2304], P(('exp', 'seq')), may hold values from -0.21875 to 0.21875
- attn_out: bfloat16 [768, 768], P(('exp', 'seq')), may hold values from -1.75 to 1.75
- gain_ffn: bfloat16 [768], P(('exp', 'seq')), may hold values from 0.099609375 to 1.8984375
- router: bfloat16 [768, 16], P(('exp', 'seq')), may hold values from -0.15917969 to 0.15917969
- expert_in: bfloat16 [16, 768, 3072], P('exp', None, 'seq'), may hold values from -0.21875 to 0.21875
- expert_out: bfloat16 [16, 3072, 768], P('exp', 'seq'), may hold values from -0.15625 to 0.15625
- cotangent: bfloat16 [8192, 768], P(('exp', 'seq')), may hold values from -6 to 6
Outputs:
- mixed_out: bfloat16 [8192, 768], P(('exp', 'seq'))
- grad_tokens: float32 [8192, 768], P(('exp', 'seq'))
- grad_gain_attn: float32 [768], P(('exp', 'seq'))
- grad_attn_in: float32 [768, 2304], P(('exp', 'seq'))
- grad_attn_out: float32 [768, 768], P(('exp', 'seq'))
- grad_gain_ffn: float32 [768], P(('exp', 'seq'))
- grad_router: float32 [768, 16], P(('exp', 'seq'))
- grad_expert_in: float32 [16, 768, 3072], P('exp', None, 'seq')
- grad_expert_out: float32 [16, 3072, 768], P('exp', 'seq')
The draws below stay inside these ranges and needn't reach their ends.
Inputs may be any that keep to these rules, and one draw needn't show every extreme that they name: `segments`: segment numbers never fall along a sequence of 1024 tokens and start at 0 in each sequence; in every draw some sequence reaches the largest number. `expert_ids`: each row names two different experts; among the rows of one device (256 aligned rows) no expert is named more than 39 times, and in some of these blocks one is named exactly 39 times.
All inputs are finite; a program needn't handle non-finite values.
Results may differ from the reference program's by a relative error of at most 0.014.
Values may be sent and summed in bfloat16 or wider, within the bound.
A program may use at most 256 MiB of HBM per device.

```python
import math
import jax
import jax.numpy as jnp
import numpy as np
from jax import lax

D = 768
HEADS = 12
HEAD_DIM = 64
FF = 3072
TOK_DEV = 256
EXPERTS = 16
SEQ_LEN = 1024
TOKENS = 8192
CAP = 39
DEVICES = 32


def draw_segments(key, part):
    key = jax.random.fold_in(key, 11)
    seq_rows = TOKENS // SEQ_LEN
    sub_keys = jax.random.split(key, 4)
    dense_row = jax.random.randint(sub_keys[3], (1, 1), 0, seq_rows)
    is_dense = jnp.arange(seq_rows, dtype=jnp.int32)[:, None] == dense_row
    doc_start = jax.random.randint(sub_keys[0], (seq_rows, 1), 1, TOK_DEV)
    doc_stop = jax.random.randint(sub_keys[1], (seq_rows, 1), SEQ_LEN - TOK_DEV + 1, SEQ_LEN)
    doc_start = jnp.where(is_dense, TOK_DEV - 1, doc_start)
    doc_stop = jnp.where(is_dense, SEQ_LEN - TOK_DEV + 1, doc_stop)
    boundary_roll = jax.random.randint(sub_keys[2], (seq_rows, SEQ_LEN), 0, 48)
    boundary_roll = jnp.where(is_dense, 0, boundary_roll)
    token_place = jnp.arange(SEQ_LEN, dtype=jnp.int32)[None, :]
    outside = (token_place < doc_start) | (token_place > doc_stop)
    boundary = (token_place == doc_start) | (token_place == doc_stop) | outside & (boundary_roll == 0) & (token_place > 0)
    return jnp.cumsum(boundary.astype(jnp.int32), axis=1).astype(jnp.int32).reshape(TOKENS)


def steps_of(own_key, dims, cuts, low, high):
    def one(dim, blocks):
        draws = jax.random.uniform(jax.random.fold_in(jax.random.fold_in(own_key, 6), dim), (blocks,), jnp.float32, low / len(cuts), high / len(cuts))
        return jnp.repeat(jnp.exp(draws), dims[dim] // blocks).reshape((-1,) + (1,) * (len(dims) - dim - 1))

    level = one(*cuts[0])
    for cut in cuts[1:]:
        level = level * one(*cut)
    return level


def shared_out(stream_key, own, number, rows, count, top, most, lean):
    ranking = jax.random.permutation(stream_key, count)
    crowded, common = shares(count, rows * top, most, lean, True), shares(count, rows * top, most, lean, False)
    places = jnp.arange(count)

    def named(lengths, turn):
        used = int((lengths > 0).sum())
        fixed = max(1, used // 4)
        shifted = fixed + (places - fixed + turn * (used - fixed)) % max(1, count - fixed)
        return jnp.zeros((count,), jnp.int32).at[ranking[jnp.where(places < fixed, places, shifted)]].set(jnp.asarray(lengths, jnp.int32))

    lengths = jnp.where(number % 4 == 0, named(crowded, number // 4), named(common, number - number // 4 - 1))
    mixed = jax.random.permutation(jax.random.fold_in(own, 3), count)
    donor, receiver = mixed[0:count // 2 * 2:2], mixed[1:count // 2 * 2:2]
    slack = jnp.minimum(lengths[donor] - 1, most - lengths[receiver]) // 2
    slack = jnp.where((donor == ranking[0]) | (receiver == ranking[0]) | (lengths[receiver] == 0), 0, jnp.maximum(slack, 0))
    shifted = jax.random.randint(jax.random.fold_in(own, 4), (count // 2,), 0, 1 << 20) % (slack + 1)
    lengths = lengths.at[donor].add(-shifted).at[receiver].add(shifted)
    items = jnp.searchsorted(jnp.cumsum(lengths), jnp.arange(rows * top), side="right").astype(jnp.int32)
    listing = items.reshape(top, rows).T
    listing = listing[jax.random.permutation(jax.random.fold_in(own, 1), rows)]
    turn = jax.random.randint(jax.random.fold_in(own, 2), (rows, 1), 0, top)
    return jnp.take_along_axis(listing, (jnp.arange(top)[None, :] + turn) % top, axis=1)


def shares(amount, total, reach, lean, full):
    portions = [(1 << 20) // math.isqrt(standing ** lean) + 1 for standing in range(1, amount + 1)]
    largest = reach if full else min(reach, max(-(-total // amount), total * portions[0] // sum(portions)))
    least = 1 if total - largest >= amount - 1 else 0
    holding, spare = [largest] + [least] * (amount - 1), total - largest - least * (amount - 1)
    while spare > 0:
        candidates = [i for i in range(1, amount) if holding[i] < largest] or [i for i in range(1, amount) if holding[i] < reach]
        mass, remaining = sum([portions[i] for i in candidates]), spare
        for i in candidates:
            extra = min(reach - holding[i], max(1, remaining * portions[i] // mass), spare)
            holding[i] = holding[i] + extra
            spare = spare - extra
    return np.array(holding)


def noise(rng, extent, scale, reach, pieces=(), held_as=jnp.bfloat16):
    values = scale * jax.random.normal(rng, extent, jnp.float32)
    if pieces:
        values = values * steps_of(rng, extent, pieces, -0.22, 0.18)
    return jnp.clip(values, -reach, reach).astype(held_as)


def setup_inputs(seed: int = 0) -> dict:
    key_list = jax.random.split(jax.random.key(seed), 12)
    tokens = noise(key_list[0], (TOKENS, D), 1.0, 6.0, ((0, 32),))
    segments = draw_segments(jax.random.fold_in(key_list[11], 71), 0)
    expert_ids_keys = jax.random.split(jax.random.fold_in(key_list[2], 1), TOKENS // TOK_DEV)
    expert_ids_turns = jax.random.permutation(jax.random.fold_in(key_list[2], 3), TOKENS // TOK_DEV)
    expert_ids = jax.vmap(lambda own, number: shared_out(jax.random.fold_in(key_list[2], 2), own, number, TOK_DEV, EXPERTS, 2, CAP, 1))(expert_ids_keys, expert_ids_turns).reshape((TOKENS, 2))
    gain_attn = jnp.clip(1.0 + 0.18 * jax.random.normal(key_list[3], (D,), jnp.float32), 0.099609375, 1.8984375).astype(jnp.bfloat16)
    attn_in = noise(key_list[4], (D, 3 * D), D ** -0.5, 0.21875, ((0, 32),))
    attn_out = noise(key_list[5], (D, D), (D // 64) ** -0.5, 1.75, ((0, 32),))
    gain_ffn = jnp.clip(1.0 + 0.18 * jax.random.normal(key_list[6], (D,), jnp.float32), 0.099609375, 1.8984375).astype(jnp.bfloat16)
    router = noise(key_list[7], (D, EXPERTS), 0.027, 0.15917969, ((0, 32),))
    expert_in = noise(key_list[8], (EXPERTS, D, FF), D ** -0.5, 0.21875, ((0, 8), (2, 4)))
    expert_out = noise(key_list[9], (EXPERTS, FF, D), (FF // 2) ** -0.5, 0.15625, ((0, 8), (1, 4)))
    cotangent = noise(key_list[10], (TOKENS, D), 1.0, 6.0, ((0, 32),))
    return {"tokens": tokens, "segments": segments, "expert_ids": expert_ids, "gain_attn": gain_attn, "attn_in": attn_in, "attn_out": attn_out, "gain_ffn": gain_ffn, "router": router, "expert_in": expert_in, "expert_out": expert_out, "cotangent": cotangent}


HIGHEST = lax.Precision.HIGHEST
EPSILON = 1e-06

@jax.custom_vjp
def low(v):
    return lax.optimization_barrier(v.astype(jnp.bfloat16)).astype(jnp.float32)

@jax.custom_vjp
def low_back(v):
    return v

def low_keep(v):
    return (low(v), None)

def low_pass(kept, grad):
    return (grad,)

def back_keep(v):
    return (v, None)

def back_low(kept, grad):
    return (low(grad),)
low.defvjp(low_keep, low_pass)
low_back.defvjp(back_keep, back_low)

def rms_norm(values, gain_values):
    return values * lax.rsqrt(lax.optimization_barrier(jnp.mean(values * values, axis=-1, keepdims=True)) + EPSILON) * gain_values

def attend_sequence(operands):
    queries, key_rows, values_seq, segment_ids = operands
    row_block = min(512, SEQ_LEN)
    key_place = jnp.arange(SEQ_LEN, dtype=jnp.int32)

    def one_block(first_row):
        query_rows = lax.dynamic_slice_in_dim(queries, first_row, row_block, 0)
        query_segments = lax.dynamic_slice_in_dim(segment_ids, first_row, row_block, 0)
        query_place = first_row + jnp.arange(row_block, dtype=jnp.int32)
        scores = low_back(jnp.einsum('qhd,khd->hqk', query_rows, key_rows, precision=HIGHEST) * HEAD_DIM ** (-0.5))
        visible = (key_place[None, :] <= query_place[:, None]) & (segment_ids[None, :] == query_segments[:, None])
        scores = jnp.where(visible[None, :, :], scores, -1e+30)
        weights = low(jax.nn.softmax(scores, axis=-1))
        return jnp.einsum('hqk,khd->qhd', weights, values_seq, precision=HIGHEST)
    firsts = jnp.arange(0, SEQ_LEN, row_block, dtype=jnp.int32)
    outputs = lax.map(jax.checkpoint(one_block), firsts)
    return outputs.reshape(SEQ_LEN, HEADS * HEAD_DIM)

def reference(tokens, segments, expert_ids, gain_attn, attn_in, attn_out, gain_ffn, router, expert_in, expert_out, cotangent):
    id_blocks = expert_ids.reshape(DEVICES, 2 * TOK_DEV)
    one_hot = (id_blocks[:, :, None] == jnp.arange(EXPERTS, dtype=jnp.int32)[None, None, :]).astype(jnp.int32)
    slot_rank = lax.optimization_barrier(jnp.sum((jnp.cumsum(one_hot, axis=1) - one_hot) * one_hot, axis=2)).astype(jnp.int32)
    per_expert = DEVICES * CAP
    device_ids = jnp.arange(DEVICES, dtype=jnp.int32)[:, None]
    slot_index = (id_blocks * per_expert + device_ids * CAP + slot_rank).reshape(-1).astype(jnp.int32)
    token_ids = jnp.repeat(jnp.arange(TOKENS, dtype=jnp.int32), 2)
    slot_table = jnp.full((EXPERTS * per_expert,), TOKENS, jnp.int32).at[slot_index].set(token_ids)
    slot_table = slot_table.reshape(EXPERTS, per_expert)
    sequence_ids = segments.reshape(TOKENS // SEQ_LEN, SEQ_LEN)
    head_shape = (TOKENS // SEQ_LEN, SEQ_LEN, HEADS, HEAD_DIM)

    def forward(inputs, gain_one, w_qkv, w_output, gain_two, w_router, w_first, w_second):
        normed_low = low(rms_norm(inputs, gain_one))
        qkv_all = low_back(low(jnp.dot(normed_low, w_qkv, precision=HIGHEST)))
        queries = qkv_all[:, :D].reshape(head_shape)
        key_rows = qkv_all[:, D:2 * D].reshape(head_shape)
        value_rows = qkv_all[:, 2 * D:].reshape(head_shape)
        attended = lax.map(attend_sequence, (queries, key_rows, value_rows, sequence_ids)).reshape(TOKENS, D)
        attended_low = low_back(low(attended))
        hidden_state = inputs + low_back(jnp.dot(attended_low, w_output, precision=HIGHEST))
        routed = low(rms_norm(hidden_state, gain_two))
        logits = jnp.dot(routed, w_router, precision=HIGHEST)
        gate_values = jax.nn.softmax(jnp.take_along_axis(logits, expert_ids, axis=1), axis=-1)
        padded = jnp.concatenate([routed, jnp.zeros((1, D), jnp.float32)], axis=0)

        def expert_rows(expert_item):
            first_weight, second_weight, row_ids = expert_item
            pre_act = low_back(jnp.dot(padded[row_ids], first_weight, precision=HIGHEST))
            activated = low(jax.nn.gelu(pre_act))
            return low_back(low(jnp.dot(activated, second_weight, precision=HIGHEST)))
        result = lax.map(jax.checkpoint(expert_rows), (w_first, w_second, slot_table))
        picked = result.reshape(EXPERTS * per_expert, D)[slot_index].reshape(TOKENS, 2, D)
        return hidden_state + lax.optimization_barrier(jnp.sum(gate_values[:, :, None] * picked, axis=1))
    mixed, backward = jax.vjp(forward, tokens.astype(jnp.float32), gain_attn.astype(jnp.float32), attn_in.astype(jnp.float32), attn_out.astype(jnp.float32), gain_ffn.astype(jnp.float32), router.astype(jnp.float32), expert_in.astype(jnp.float32), expert_out.astype(jnp.float32))
    gradients = backward(cotangent.astype(jnp.float32))
    return (mixed.astype(jnp.bfloat16), gradients[0], gradients[1], gradients[2], gradients[3], gradients[4], gradients[5], gradients[6], gradients[7])
```

```python
import math

import jax
import jax.numpy as jnp
from jax import lax
from jax.experimental import pallas as pl
from jax.experimental.pallas import tpu as pltpu
from jax.sharding import PartitionSpec as P

HEAD_DIM = 64


EPSILON = 1e-06
MASKED = -1e30
HIGHEST = lax.Precision.HIGHEST


def contract_rows(first_operand, second_operand):
    return lax.dot_general(
        first_operand, second_operand, (((0,), (0,)), ((), ())), preferred_element_type=jnp.float32
    )


def contract_cols(first_operand, second_operand):
    return lax.dot_general(
        first_operand, second_operand, (((1,), (1,)), ((), ())), preferred_element_type=jnp.float32
    )


def norm_forward(values, gain_values):
    inverse = lax.rsqrt(jnp.mean(values * values, axis=-1, keepdims=True) + EPSILON)
    return (values * inverse * gain_values.astype(jnp.float32), inverse)


def norm_backward(values, inverse, gain_values, upstream):
    scaled = upstream * gain_values.astype(jnp.float32)
    gain_grad = jnp.sum(upstream * values * inverse, axis=0)
    value_grad = inverse * scaled - values * inverse**3 * jnp.mean(
        scaled * values, axis=-1, keepdims=True
    )
    return (value_grad, gain_grad)


BLOCK_ROWS = 256
VMEM_BYTES = 40 * 1024 * 1024


def head_softmax(qkv_ref, col_ref, row_ref, own_cols, head_index, first_row, rows):
    stop = first_row + rows
    first_col = head_index * HEAD_DIM
    query = qkv_ref[first_row:stop, first_col : first_col + HEAD_DIM]
    key = qkv_ref[0:stop, own_cols + first_col : own_cols + first_col + HEAD_DIM]
    value = qkv_ref[0:stop, 2 * own_cols + first_col : 2 * own_cols + first_col + HEAD_DIM]
    query_place = first_row + lax.broadcasted_iota(jnp.int32, (rows, stop), 0)
    key_place = lax.broadcasted_iota(jnp.int32, (rows, stop), 1)
    visible = (key_place <= query_place) & (col_ref[first_row:stop, :] == row_ref[:, 0:stop])
    scores = contract_cols(query, key) * (1.0 / math.sqrt(HEAD_DIM))
    scores = jnp.where(visible, scores, MASKED)
    shifted = jnp.exp(scores - jnp.max(scores, axis=1, keepdims=True))
    weights = shifted / jnp.sum(shifted, axis=1, keepdims=True)
    return query, key, value, weights


def attend_kernel(qkv_ref, col_ref, row_ref, out_ref):
    own_cols = out_ref.shape[1]
    rows = min(BLOCK_ROWS, out_ref.shape[0])
    for first_row in range(0, out_ref.shape[0], rows):
        pieces = []
        for head_index in range(own_cols // HEAD_DIM):
            _, _, value, weights = head_softmax(
                qkv_ref, col_ref, row_ref, own_cols, head_index, first_row, rows
            )
            pieces.append(
                jnp.dot(weights.astype(jnp.bfloat16), value, preferred_element_type=jnp.float32)
            )
        out_ref[first_row : first_row + rows, :] = jnp.concatenate(pieces, axis=1).astype(
            jnp.bfloat16
        )


def attend_back_kernel(qkv_ref, grad_ref, col_ref, row_ref, out_ref, key_sum, value_sum):
    own_cols = grad_ref.shape[1]
    heads = own_cols // HEAD_DIM
    total = grad_ref.shape[0]
    rows = min(BLOCK_ROWS, total)
    scale = 1.0 / math.sqrt(HEAD_DIM)
    key_sum[...] = jnp.zeros_like(key_sum)
    value_sum[...] = jnp.zeros_like(value_sum)
    for first_row in range(0, total, rows):
        stop = first_row + rows
        pieces = []
        for head_index in range(heads):
            query, key, value, weights = head_softmax(
                qkv_ref, col_ref, row_ref, own_cols, head_index, first_row, rows
            )
            first_col = head_index * HEAD_DIM
            out_grad = grad_ref[first_row:stop, first_col : first_col + HEAD_DIM]
            weight_grad = contract_cols(out_grad, value)
            row_dot = jnp.sum(weights * weight_grad, axis=1, keepdims=True)
            score_low = (weights * (weight_grad - row_dot)).astype(jnp.bfloat16)
            pieces.append(jnp.dot(score_low, key, preferred_element_type=jnp.float32) * scale)
            key_sum[head_index, 0:stop, :] += contract_rows(score_low, query)
            value_sum[head_index, 0:stop, :] += contract_rows(
                weights.astype(jnp.bfloat16), out_grad
            )
        out_ref[first_row:stop, 0:own_cols] = jnp.concatenate(pieces, axis=1).astype(jnp.bfloat16)
    sums = [key_sum[n] * scale for n in range(heads)] + [value_sum[n] for n in range(heads)]
    out_ref[:, own_cols : 3 * own_cols] = jnp.concatenate(sums, axis=1).astype(jnp.bfloat16)


def attend(qkv_own, segments):
    total, width = qkv_own.shape
    return pl.pallas_call(
        attend_kernel,
        out_shape=jax.ShapeDtypeStruct((total, width // 3), jnp.bfloat16),
        compiler_params=pltpu.CompilerParams(vmem_limit_bytes=VMEM_BYTES),
        cost_estimate=pl.CostEstimate(
            flops=total * total * width, bytes_accessed=4 * total * width, transcendentals=0
        ),
    )(qkv_own, segments[:, None], segments[None, :])


def attend_back(qkv_own, attended_grad, segments):
    total, width = qkv_own.shape
    heads = width // (3 * HEAD_DIM)
    return pl.pallas_call(
        attend_back_kernel,
        out_shape=jax.ShapeDtypeStruct((total, width), jnp.bfloat16),
        scratch_shapes=[
            pltpu.VMEM((heads, total, HEAD_DIM), jnp.float32),
            pltpu.VMEM((heads, total, HEAD_DIM), jnp.float32),
        ],
        compiler_params=pltpu.CompilerParams(vmem_limit_bytes=VMEM_BYTES),
        cost_estimate=pl.CostEstimate(
            flops=3 * total * total * width, bytes_accessed=6 * total * width, transcendentals=0
        ),
    )(qkv_own, attended_grad, segments[:, None], segments[None, :])


def on_device(
    tokens,
    segments,
    expert_ids,
    gain_attn,
    attn_in,
    attn_out,
    gain_ffn,
    router,
    expert_in,
    expert_out,
    cotangent,
):
    tok_rows, model_width = tokens.shape
    head_count = model_width // HEAD_DIM
    exp_size = lax.axis_size("exp")
    seq_size = lax.axis_size("seq")
    seq_index = lax.axis_index("seq")
    exp_index = lax.axis_index("exp")
    experts_dev = expert_in.shape[0]
    expert_total = router.shape[1]
    own_rows = attn_in.shape[0]
    capacity = max(2, 5 * tok_rows // (2 * expert_total) - 1)
    slots = -(-capacity // 8) * 8
    chunk_rows = experts_dev * slots
    own_heads = -(-head_count // seq_size)
    own_cols = own_heads * HEAD_DIM
    all_cols = own_cols * seq_size

    tokens_all = lax.all_gather(tokens, "seq", axis=0, tiled=True)
    in_pieces = jnp.pad(
        attn_in.reshape(own_rows, 3, model_width), ((0, 0), (0, 0), (0, all_cols - model_width))
    ).reshape(own_rows, 3, seq_size, own_cols)
    in_pieces = in_pieces.transpose(2, 0, 1, 3).reshape(seq_size, own_rows, 3 * own_cols)
    small = jnp.concatenate([gain_attn[:, None], gain_ffn[:, None], router], axis=1)
    packed = jnp.concatenate(
        [in_pieces, jnp.broadcast_to(small[None], (seq_size,) + small.shape)], axis=2
    )
    packed = lax.all_to_all(packed, "seq", split_axis=0, concat_axis=0, tiled=True)
    packed = lax.all_gather(
        packed.reshape(seq_size * own_rows, -1), "exp", axis=0, tiled=True
    )
    w_own = packed[:, : 3 * own_cols]
    gain_one = packed[:, 3 * own_cols]
    gain_two = packed[:, 3 * own_cols + 1]
    w_router = packed[:, 3 * own_cols + 2 :]
    w_output = lax.all_gather(attn_out, ("exp", "seq"), axis=0, tiled=True)

    flat_ids = expert_ids.reshape(-1)
    id_table = (flat_ids[:, None] == jnp.arange(expert_total, dtype=jnp.int32)[None, :]).astype(
        jnp.int32
    )
    slot_rank = jnp.sum((jnp.cumsum(id_table, axis=0) - id_table) * id_table, axis=1)
    position = flat_ids * slots + slot_rank
    other_ids = expert_ids[:, ::-1].reshape(-1, 1).astype(jnp.bfloat16)
    upstream_rows = jnp.concatenate(
        [
            jnp.repeat(cotangent, 2, axis=0),
            jnp.pad(other_ids, ((0, 0), (0, 127))),
        ],
        axis=1,
    )

    def dispatch(values):
        sent = jnp.zeros((exp_size * chunk_rows, values.shape[1]), jnp.bfloat16)
        sent = sent.at[position].set(values).reshape(exp_size, chunk_rows, values.shape[1])
        received = lax.all_to_all(sent, "exp", split_axis=0, concat_axis=0, tiled=True)
        return lax.all_gather(received, "seq", axis=0, tiled=True).reshape(
            seq_size * exp_size, experts_dev, slots, values.shape[1]
        )

    upstream_all = dispatch(upstream_rows)

    inputs = tokens.astype(jnp.float32)
    inputs_all = tokens_all.astype(jnp.float32)
    normed_all, inverse_all = norm_forward(inputs_all, gain_one)
    normed_all_low = normed_all.astype(jnp.bfloat16)
    qkv_own = jnp.dot(normed_all_low, w_own, preferred_element_type=jnp.float32).astype(
        jnp.bfloat16
    )
    attended_own = attend(qkv_own, segments)
    attended_low = lax.all_to_all(
        attended_own.reshape(seq_size, tok_rows, own_cols),
        "seq",
        split_axis=0,
        concat_axis=0,
        tiled=True,
    )
    attended_low = attended_low.transpose(1, 0, 2).reshape(tok_rows, all_cols)[:, :model_width]
    hidden_state = inputs + jnp.dot(attended_low, w_output, preferred_element_type=jnp.float32)
    normed_two, inverse_two = norm_forward(hidden_state, gain_two)
    routed_low = normed_two.astype(jnp.bfloat16)
    all_rows = dispatch(jnp.repeat(routed_low, 2, axis=0))
    logits = jnp.dot(routed_low, w_router, preferred_element_type=jnp.float32)
    chosen = (
        expert_ids[:, :, None] == jnp.arange(expert_total, dtype=jnp.int32)[None, None, :]
    ).astype(jnp.float32)
    picked = jnp.sum(chosen * logits[:, None, :], axis=2)
    gate_values = jax.nn.softmax(picked, axis=-1)

    values = []
    backs = []
    in_grads = []
    out_grads = []
    row_count = seq_size * exp_size * slots
    for local_expert in range(experts_dev):
        rows = all_rows[:, local_expert].reshape(row_count, model_width)
        upstream_ext = upstream_all[:, local_expert].reshape(row_count, -1)
        row_logits = jnp.dot(rows, w_router, preferred_element_type=jnp.float32)
        expert_range = jnp.arange(expert_total, dtype=jnp.int32)[None, :]
        here = expert_range == exp_index * experts_dev + local_expert
        there = expert_range == upstream_ext[:, model_width : model_width + 1].astype(jnp.int32)
        logit_here = jnp.sum(jnp.where(here, row_logits, 0.0), axis=1, keepdims=True)
        logit_there = jnp.sum(jnp.where(there, row_logits, 0.0), axis=1, keepdims=True)
        top = jnp.maximum(logit_here, logit_there)
        raised = jnp.exp(logit_here - top)
        row_gates = raised / (raised + jnp.exp(logit_there - top))
        row_grads = (row_gates * upstream_ext[:, :model_width].astype(jnp.float32)).astype(
            jnp.bfloat16
        )
        pre_act = jnp.dot(rows, expert_in[local_expert], preferred_element_type=jnp.float32)
        activated, gelu_back = jax.vjp(jax.nn.gelu, pre_act)
        activated_low = activated.astype(jnp.bfloat16)
        values.append(
            jnp.dot(activated_low, expert_out[local_expert], preferred_element_type=jnp.float32)
        )
        hidden_grad = contract_cols(row_grads, expert_out[local_expert])
        pre_low = gelu_back(hidden_grad)[0].astype(jnp.bfloat16)
        backs.append(contract_cols(pre_low, expert_in[local_expert]))
        out_grads.append(contract_rows(activated_low, row_grads))
        in_grads.append(contract_rows(rows, pre_low))
    grad_expert_in = jnp.stack(in_grads, axis=0)
    grad_expert_out = jnp.stack(out_grads, axis=0)

    def give_back(pieces):
        stacked = jnp.stack(
            [
                piece.astype(jnp.bfloat16).reshape(seq_size, exp_size, slots, model_width)
                for piece in pieces
            ],
            axis=2,
        ).reshape(seq_size * exp_size, chunk_rows, model_width)
        own = lax.psum_scatter(stacked, "seq", scatter_dimension=0, tiled=True)
        own = lax.all_to_all(own, "exp", split_axis=0, concat_axis=0, tiled=True)
        return (
            own.reshape(-1, model_width)[position]
            .astype(jnp.float32)
            .reshape(tok_rows, 2, model_width)
        )

    expert_float = give_back(values)
    back_float = give_back(backs)
    mixed = hidden_state + jnp.sum(gate_values[:, :, None] * expert_float, axis=1)
    upstream = cotangent.astype(jnp.float32)
    gate_grad = jnp.sum(upstream[:, None, :] * expert_float, axis=2)
    picked_grad = gate_values * (
        gate_grad - jnp.sum(gate_values * gate_grad, axis=1, keepdims=True)
    )
    logit_grad = jnp.sum(chosen * picked_grad[:, :, None], axis=1)
    router_grad = jnp.dot(routed_low.astype(jnp.float32).T, logit_grad, precision=HIGHEST)
    routed_grad = jnp.dot(logit_grad, w_router.astype(jnp.float32).T, precision=HIGHEST)
    routed_grad = routed_grad + jnp.sum(back_float, axis=1)
    state_grad, gain_two_grad = norm_backward(hidden_state, inverse_two, gain_two, routed_grad)
    state_grad = state_grad + upstream
    state_low = state_grad.astype(jnp.bfloat16)

    state_all = lax.all_gather(state_low, "seq", axis=0, tiled=True)
    output_grad = contract_rows(attended_low, state_low).astype(jnp.bfloat16)
    output_grad = lax.psum_scatter(
        output_grad, ("exp", "seq"), scatter_dimension=0, tiled=True
    ).astype(jnp.float32)
    w_output_own = lax.dynamic_slice_in_dim(
        jnp.pad(w_output, ((0, all_cols - model_width), (0, 0))), seq_index * own_cols, own_cols
    )
    attended_grad = contract_cols(state_all, w_output_own).astype(jnp.bfloat16)
    qkv_grad = attend_back(qkv_own, attended_grad, segments)
    normed_part = contract_cols(qkv_grad, w_own)
    normed_grad = lax.psum_scatter(
        normed_part.astype(jnp.bfloat16), "seq", scatter_dimension=0, tiled=True
    ).astype(jnp.float32)
    weight_part = contract_rows(normed_all_low, qkv_grad)
    gain_one_part = jnp.sum(normed_part * inputs_all * inverse_all, axis=0)
    grad_pack = jnp.concatenate(
        [weight_part, gain_one_part[:, None], gain_two_grad[:, None], router_grad], axis=1
    ).astype(jnp.bfloat16)
    grad_pack = lax.all_to_all(
        grad_pack.reshape(exp_size, seq_size * own_rows, -1),
        "exp",
        split_axis=0,
        concat_axis=0,
        tiled=True,
    )
    grad_pack = jnp.sum(grad_pack.astype(jnp.float32), axis=0)
    grad_pack = lax.all_to_all(
        grad_pack.reshape(seq_size, own_rows, -1), "seq", split_axis=0, concat_axis=0, tiled=True
    )
    weight_grad = grad_pack[:, :, : 3 * own_cols].reshape(seq_size, own_rows, 3, own_cols)
    weight_grad = weight_grad.transpose(1, 2, 0, 3).reshape(own_rows, 3, all_cols)
    weight_grad = weight_grad[:, :, :model_width].reshape(own_rows, 3 * model_width)
    small_grad = jnp.sum(grad_pack[:, :, 3 * own_cols :], axis=0)

    first = seq_index * tok_rows
    inverse_one = lax.dynamic_slice_in_dim(inverse_all, first, tok_rows)
    input_part, _ = norm_backward(inputs, inverse_one, gain_one, normed_grad)
    input_grad = state_grad + input_part
    return (
        mixed.astype(jnp.bfloat16),
        input_grad,
        small_grad[:, 0],
        weight_grad,
        output_grad,
        small_grad[:, 1],
        small_grad[:, 2:],
        grad_expert_in,
        grad_expert_out,
    )


def solution(mesh):
    return jax.shard_map(
        on_device,
        mesh=mesh,
        in_specs=(
            P(("exp", "seq"), None),
            P("exp"),
            P(("exp", "seq"), None),
            P(("exp", "seq")),
            P(("exp", "seq"), None),
            P(("exp", "seq"), None),
            P(("exp", "seq")),
            P(("exp", "seq"), None),
            P("exp", None, "seq"),
            P("exp", "seq", None),
            P(("exp", "seq"), None),
        ),
        out_specs=(
            P(("exp", "seq"), None),
            P(("exp", "seq"), None),
            P(("exp", "seq")),
            P(("exp", "seq"), None),
            P(("exp", "seq"), None),
            P(("exp", "seq")),
            P(("exp", "seq"), None),
            P("exp", None, "seq"),
            P("exp", "seq", None),
        ),
        check_vma=False,
    )
```
